32 devices in a mesh: tm: 8 (over y, x, core), freq: 4 (over z).
Axes of the slice: x: 2, y: 2, z: 4, core: 2. Of those that a mesh axis runs over, the one named last changes fastest.
Arguments:
- visibility: bfloat16 [2, 16, 512, 2048], P(None, None, 'freq', 'tm'), may hold values from -6 to 6
- spectrum_power_sum: float32 [512, 2048], P('freq', 'tm'), may hold values from 50 to 500, as said below
- square_sum: float32 [512, 2048], P('freq', 'tm'), as said below
- accum_count: int32 [512, 2048], P('freq', 'tm'), may hold values from 64 to 256
- rfi_mask: int32 [512, 2048], P('freq', 'tm'), may hold values 0 or 1
- baseline_delay_class: int32 [16, 1], P('freq'), may hold values from 0 to 3
- filter_bank: bfloat16 [4, 512, 512], replicated, may hold values from -0.25 to 0.25
Outputs:
- filtered: bfloat16 [2, 16, 512, 2048], P(None, 'freq', None, 'tm')
The draws below stay inside these ranges and needn't reach their ends.
Inputs may be any that keep to these rules, and one draw needn't show every extreme that they name: `spectrum_power_sum`: positive in every sample. `square_sum`: positive in every sample.
All inputs are finite; a program needn't handle non-finite values. No bound on the sum of `rfi_mask` on one device may be relied on, other than what follows from the above.
Results may differ from the reference program's by a relative error of at most 0.0043.
The reference program's roundings to bfloat16 on the way (of `weighted` and `spectrum`) count: a program that leaves them out, or rounds other values in their place, can miss the bound.
Values may be sent and summed in bfloat16 or wider, within the bound.
No kernel may reach another device: no remote copies, remote signals or barrier semaphores. Data moves between devices by JAX's collectives and lax.ppermute only.
A program may use at most 128 MiB of HBM per device.

```python
import math
import jax
import jax.numpy as jnp
from jax import lax

RIM = 16
CUTOFF_CLASSES = 4
BASELINE_COUNT = 16
FREQUENCY_COUNT = 512
SIDEREAL_COUNT = 2048


def flag_fields(key):
    count_key = jax.random.fold_in(key, 101)
    power_key = jax.random.fold_in(key, 202)
    counts = jax.random.randint(count_key, (FREQUENCY_COUNT, SIDEREAL_COUNT), 64, 257).astype(jnp.int32)
    power = jnp.exp(jax.random.uniform(power_key, (FREQUENCY_COUNT, SIDEREAL_COUNT), jnp.float32, math.log(50.0), math.log(500.0)))
    return (counts, power)


def draw_accum_count(key, part):
    counts, power = flag_fields(key)
    return counts


def draw_spectrum_power_sum(key, part):
    counts, power = flag_fields(key)
    return power


def draw_square_sum(key, part):
    counts, power = flag_fields(key)
    ratio_key = jax.random.fold_in(key, 303)
    ratio = jax.random.uniform(ratio_key, (FREQUENCY_COUNT, SIDEREAL_COUNT), jnp.float32, 1.4, 3.2)
    return power * power * ratio / counts.astype(jnp.float32)


def with_ends(values, key, smallest, high):
    longest = values.shape.index(max(values.shape))
    spots = []
    for shift in (0, 1):
        where = [jax.random.randint(jax.random.fold_in(key, axis), (), 0, length) for axis, length in enumerate(values.shape)]
        where[longest] = (where[longest] + shift) % values.shape[longest]
        spots.append(tuple(where))
    return values.at[spots[0]].set(smallest).at[spots[1]].set(high)


def shard_levels(own_key, shape, pieces, low, largest):
    loudness, own = 1.0, jax.random.fold_in(own_key, 6)
    for position, blocks in pieces:
        heights = jnp.exp(jax.random.uniform(jax.random.fold_in(own, position), (blocks,), jnp.float32, low / len(pieces), largest / len(pieces)))
        loudness = loudness * jnp.repeat(heights, shape[position] // blocks).reshape([-1 if axis == position else 1 for axis in range(len(shape))])
    return loudness


def different_ones(own_key, rows, amount, top, lift):
    sequence = jax.random.permutation(jax.random.fold_in(own_key, 1), amount)
    boost = sequence
    for power in range(3):
        boost = boost * boost // amount
    boost = boost * lift // amount
    lots = jax.random.randint(jax.random.fold_in(own_key, 2), (rows, amount), 0, 4096) + boost
    fixed_rows = jax.random.permutation(jax.random.fold_in(own_key, 3), rows)[jnp.arange(amount) % rows]
    lots = jnp.where(jnp.arange(rows)[:, None] == fixed_rows[None, :], 1 << 14, lots)
    score = lots * amount + jnp.arange(amount)
    return lax.top_k(score.astype(jnp.int32), top)[1].astype(jnp.int32)


def noise(own_key, extent, spread, reach, cuts=(), held_as=jnp.bfloat16):
    values = spread * jax.random.normal(own_key, extent, jnp.float32)
    if cuts:
        values = values * shard_levels(own_key, extent, cuts, -0.22, 0.18)
    return jnp.clip(values, -reach, reach).astype(held_as)


def setup_inputs(seed: int = 0) -> dict:
    arg_keys = jax.random.split(jax.random.key(seed), 8)
    return {
        "visibility": noise(arg_keys[0], (2, BASELINE_COUNT, FREQUENCY_COUNT, SIDEREAL_COUNT), 1.0, 6.0, ((2, 4), (3, 8))),
        "spectrum_power_sum": draw_spectrum_power_sum(jax.random.fold_in(arg_keys[7], 71), 0),
        "square_sum": draw_square_sum(jax.random.fold_in(arg_keys[7], 71), 0),
        "accum_count": draw_accum_count(jax.random.fold_in(arg_keys[7], 71), 0),
        "rfi_mask": with_ends((jax.random.randint(arg_keys[4], (FREQUENCY_COUNT, SIDEREAL_COUNT), 0, 10) < 9).astype(jnp.int32), jax.random.fold_in(arg_keys[4], 1), 0, 1),
        "baseline_delay_class": different_ones(arg_keys[5], BASELINE_COUNT, CUTOFF_CLASSES, 1, 2048),
        "filter_bank": noise(arg_keys[6], (CUTOFF_CLASSES, FREQUENCY_COUNT, FREQUENCY_COUNT), FREQUENCY_COUNT ** -0.5, 0.25),
    }


def smooth_periodic(flag_weight):
    total = jnp.zeros(flag_weight.shape, jnp.float32)
    for offset in range(2 * RIM + 1):
        factor = (RIM + 1 - abs(offset - RIM)) / float((RIM + 1) ** 2)
        total = total + factor * jnp.roll(flag_weight, RIM - offset, axis=1)
    return total

def reference(visibility, spectrum_power_sum, square_sum, accum_count, rfi_mask, baseline_delay_class, filter_bank):
    counts = accum_count.astype(jnp.float32)
    kurtosis = (counts + 1.0) / (counts - 1.0) * (counts * square_sum / (spectrum_power_sum * spectrum_power_sum) - 1.0)
    flag_weight = rfi_mask.astype(jnp.float32) * jnp.exp(-2.0 * (kurtosis - 1.0) ** 2)
    smooth_weight = smooth_periodic(flag_weight)
    norm_scale = 1.0 / math.sqrt(SIDEREAL_COUNT)

    def per_baseline(inputs):
        vis_one, class_one = inputs
        weighted = (vis_one.astype(jnp.float32) * smooth_weight[None]).astype(jnp.bfloat16)
        widened = weighted.astype(jnp.float32)
        transformed = jnp.fft.fft(widened[0] + 1j * widened[1], axis=-1) * norm_scale
        spectrum = jnp.stack([jnp.real(transformed), jnp.imag(transformed)]).astype(jnp.bfloat16)
        matrix = lax.dynamic_index_in_dim(filter_bank, class_one[0].astype(jnp.int32), 0, keepdims=False)
        first = jnp.dot(matrix, spectrum[0], preferred_element_type=jnp.float32)
        second = jnp.dot(matrix, spectrum[1], preferred_element_type=jnp.float32)
        return jnp.stack([first, second]).astype(jnp.bfloat16)
    result = lax.map(per_baseline, (jnp.moveaxis(visibility, 1, 0), baseline_delay_class))
    return jnp.moveaxis(result, 0, 1)
```

```python
import functools
import math

import jax
import jax.numpy as jnp
import ml_dtypes
import numpy as np
from jax import lax
from jax.experimental import pallas as pl
from jax.experimental.pallas import tpu as pltpu
from jax.sharding import PartitionSpec as P

RIM = 16
LANES = 128
VMEM_BYTES = 48 * 1024 * 1024

WHOLE = pl.BlockSpec(memory_space=pltpu.VMEM)
SCALARS = pl.BlockSpec(memory_space=pltpu.SMEM)


def row_type(rows):
    return jnp.bfloat16 if rows % 16 == 0 else jnp.float32


def params():
    return pltpu.CompilerParams(vmem_limit_bytes=VMEM_BYTES)


def cost(flops, arrays):
    return pl.CostEstimate(flops=flops, bytes_accessed=sum(a.size * a.dtype.itemsize for a in arrays), transcendentals=0)


def swap(value, axis, k):
    size = lax.axis_size(axis)
    return lax.ppermute(value, axis, [(i, i ^ k) for i in range(size)])


def exchange(blocks, axis):
    order = sorted(range(1, len(blocks)), key=lambda k: (-bin(k >> 1).count("1"), k))
    moved = {0: blocks[0]}
    for k in order:
        moved[k] = swap(blocks[k], axis, k)
    return [moved[k] for k in range(len(blocks))]


def smoothing_weights(spectrum_power_sum, square_sum, accum_count, rfi_mask):
    counts = accum_count.astype(jnp.float32)
    kurtosis = (
        (counts + 1.0)
        / (counts - 1.0)
        * (counts * square_sum / (spectrum_power_sum * spectrum_power_sum) - 1.0)
    )
    flag_weight = rfi_mask.astype(jnp.float32) * jnp.exp(-2.0 * (kurtosis - 1.0) ** 2)
    devices, length = lax.axis_size("tm"), flag_weight.shape[1]
    up = [(i, (i + 1) % devices) for i in range(devices)]
    before = lax.ppermute(flag_weight[:, length - RIM :], "tm", up)
    after = lax.ppermute(flag_weight[:, :RIM], "tm", [(j, i) for i, j in up])
    padded = jnp.concatenate([before, flag_weight, after], axis=1)
    smooth_weight = jnp.zeros(flag_weight.shape, jnp.float32)
    for offset in range(2 * RIM + 1):
        factor = (RIM + 1 - abs(offset - RIM)) / float((RIM + 1) ** 2)
        smooth_weight = smooth_weight + factor * padded[:, offset : offset + length]
    return smooth_weight


def weigh_by_baseline(here, vis, smooth, *outs):
    me = here[1]
    for k, out in enumerate(outs):
        dest = me ^ k
        for c in range(2):
            for b in range(vis.shape[3]):
                out[c, b] = (vis[c, dest, 0, b].astype(jnp.float32) * smooth[...]).astype(jnp.bfloat16)


def weigh_by_channel(here, vis, smooth, *outs):
    me = here[0]
    fs = vis.shape[4] // len(outs)
    for k, out in enumerate(outs):
        rows = pl.ds(pl.multiple_of((me ^ k) * fs, fs), fs)
        part = smooth[rows, :]
        for c in range(2):
            for z in range(vis.shape[1]):
                for b in range(vis.shape[3]):
                    out[c, z * vis.shape[3] + b] = (vis[c, z, 0, b, rows, :].astype(jnp.float32) * part).astype(jnp.bfloat16)


def weigh(kernel, here, vis, smooth, half, shapes):
    parts, z, _, hb, fl, length = vis.shape
    block = pl.BlockSpec((parts, z, 1, hb, fl, length), lambda i: (0, 0, half, 0, 0, 0))
    fixed = pl.BlockSpec((fl, length), lambda i: (0, 0))
    outs = [jax.ShapeDtypeStruct(s, jnp.bfloat16) for s in shapes]
    return pl.pallas_call(
        kernel,
        grid=(1,),
        out_shape=outs,
        in_specs=[SCALARS, block, fixed],
        out_specs=[pl.BlockSpec(s, lambda i: (0, 0, 0, 0)) for s in shapes],
        compiler_params=params(),
        cost_estimate=cost(0, outs + outs),
    )(here, vis, smooth)


def channels_to_baselines(here, *refs, z_count):
    n = len(refs) - z_count
    ins, outs = refs[:n], refs[n:]
    fs, hb = ins[0].shape[2], outs[0].shape[1]
    for kz, out in enumerate(outs):
        dest = here[1] ^ kz
        for k, block in enumerate(ins):
            rows = pl.ds(pl.multiple_of((here[0] ^ k) * fs, fs), fs)
            for c in range(2):
                for b in range(hb):
                    out[c, b, rows, :] = block[c, dest * hb + b]


def baselines_to_channels(here, *refs, z_count):
    ins, outs = refs[:z_count], refs[z_count:]
    fs, hb = outs[0].shape[2], ins[0].shape[1]
    for k, out in enumerate(outs):
        rows = pl.ds(pl.multiple_of((here[0] ^ k) * fs, fs), fs)
        for kz, block in enumerate(ins):
            source = here[1] ^ kz
            for c in range(2):
                for b in range(hb):
                    out[c, source * hb + b] = block[c, b, rows, :]


def repack(kernel, here, blocks, shapes, z_count):
    outs = [jax.ShapeDtypeStruct(s, jnp.bfloat16) for s in shapes]
    return pl.pallas_call(
        functools.partial(kernel, z_count=z_count),
        out_shape=outs,
        in_specs=[SCALARS] + [WHOLE] * len(blocks),
        out_specs=[WHOLE] * len(outs),
        compiler_params=params(),
        cost_estimate=cost(0, list(blocks) + outs),
    )(here, *blocks)


def transform_tables(n, length):
    group = length // n
    lane = np.arange(length)
    order = np.zeros((length, length))
    order[lane, (lane % n) * group + lane // n] = 1.0
    angle = 2.0 * np.pi / length * (np.outer(lane, lane) % length)
    cosine, sine = np.cos(angle), np.sin(angle)
    table = np.block([[cosine, -sine], [sine, cosine]])
    high = table.astype(ml_dtypes.bfloat16)
    low = (table - high.astype(np.float64)).astype(ml_dtypes.bfloat16)
    turn = 2.0 * np.pi / (n * length) * np.outer(np.arange(n), lane)
    scale = 1.0 / math.sqrt(n * length)
    twiddle = np.stack([np.cos(turn), np.sin(turn)]) * scale
    return order.astype(ml_dtypes.bfloat16), high, low, twiddle.astype(np.float32)


def short_dft(values):
    n = len(values)
    if n == 1:
        return values
    even, odd = short_dft(values[0::2]), short_dft(values[1::2])
    out = [None] * n
    for k in range(n // 2):
        real, imag = odd[k]
        if 4 * k == n:
            real, imag = imag, -real
        elif k:
            c, s = math.cos(2.0 * math.pi * k / n), math.sin(2.0 * math.pi * k / n)
            if 8 * k == n:
                real, imag = c * (real + imag), c * (imag - real)
            elif 8 * k == 3 * n:
                real, imag = s * (imag - real), -s * (real + imag)
            else:
                real, imag = c * real + s * imag, c * imag - s * real
        out[k] = (even[k][0] + real, even[k][1] + imag)
        out[k + n // 2] = (even[k][0] - real, even[k][1] - imag)
    return out


def transpose_groups(values, group):
    values, n = [list(v) for v in values], len(values)
    lane = lax.broadcasted_iota(jnp.int32, values[0][0].shape, 1)
    bit = n // 2
    while bit:
        shift = bit * group
        for i in range(n):
            if i & bit:
                continue
            a, b = values[i], values[i + bit]
            if shift >= LANES:
                step = shift // LANES
                for col in range(len(a)):
                    if not col & step:
                        a[col + step], b[col] = b[col], a[col + step]
            else:
                upper = (lane & shift) != 0
                for col in range(len(a)):
                    x, y = a[col], b[col]
                    a[col] = jnp.where(upper, pltpu.roll(y, shift, 1), x)
                    b[col] = jnp.where(upper, y, pltpu.roll(x, LANES - shift, 1))
        bit //= 2
    return values


def transform(here, order, high, low, twiddle, *refs, n):
    ins, outs = refs[:n], refs[n : 2 * n]
    ordered, lined, stage, done = refs[2 * n :]
    me = here[0]
    parts, planes, fs, length = ins[0].shape
    group, cols = length // n, length // LANES
    per = lined.shape[1] // fs

    def step(i, carry):
        for c in range(parts):
            for k in range(n):
                block = ins[k][c, pl.ds(i * per, per)].reshape(per * fs, length)
                ordered[me ^ k] = jnp.dot(block, order[...], preferred_element_type=jnp.float32)
            for r in range(0, per * fs, 16):
                values = [[ordered[p, r : r + 16, q * LANES : (q + 1) * LANES] for q in range(cols)] for p in range(n)]
                for v, columns in enumerate(transpose_groups(values, group)):
                    for q, column in enumerate(columns):
                        lined[v, r : r + 16, c * length + q * LANES : c * length + (q + 1) * LANES] = column.astype(jnp.bfloat16)
        flat = lined[...].reshape(n * per * fs, 2 * length)
        total = jnp.dot(flat, high[...], preferred_element_type=jnp.float32)
        total = total + jnp.dot(flat, low[...], preferred_element_type=jnp.float32)
        stage[...] = total.reshape(n, per * fs, 2 * length)
        for r in range(0, per * fs, 16):
            for q in range(cols):
                first, second = slice(q * LANES, (q + 1) * LANES), slice(length + q * LANES, length + (q + 1) * LANES)
                turned = []
                for v in range(n):
                    real, imag = stage[v, r : r + 16, first], stage[v, r : r + 16, second]
                    c, s = twiddle[0, v : v + 1, first], twiddle[1, v : v + 1, first]
                    turned.append((real * c + imag * s, imag * c - real * s))
                for m, pair in enumerate(short_dft(turned)):
                    for c in range(2):
                        done[m, c, r : r + 16, first] = pair[c].astype(jnp.bfloat16)
        for k in range(n):
            for c in range(2):
                outs[k][c, pl.ds(i * per, per)] = done[me ^ k, c].reshape(per, fs, length)
        return carry

    lax.fori_loop(0, planes // per, step, 0)


def transform_call(here, blocks):
    n = len(blocks)
    parts, planes, fs, length = blocks[0].shape
    per = math.gcd(planes, 4)
    rows = per * fs
    tables = transform_tables(n, length)
    outs = [jax.ShapeDtypeStruct(b.shape, jnp.bfloat16) for b in blocks]
    return pl.pallas_call(
        functools.partial(transform, n=n),
        out_shape=outs,
        in_specs=[SCALARS] + [WHOLE] * (4 + n),
        out_specs=[WHOLE] * n,
        scratch_shapes=[
            pltpu.VMEM((n, rows, length), jnp.float32),
            pltpu.VMEM((n, rows, 2 * length), jnp.bfloat16),
            pltpu.VMEM((n, rows, 2 * length), jnp.float32),
            pltpu.VMEM((n, 2, rows, length), jnp.bfloat16),
        ],
        compiler_params=params(),
        cost_estimate=cost(4 * n * planes * fs * (2 * length) ** 2, list(blocks) + outs),
    )(here, *[jnp.asarray(t) for t in tables], *blocks)


def filter_kernel(classes, here, bank, *refs, count, from_baselines, aliased):
    ins, out, lined = refs[:count], refs[count + aliased], refs[-1]
    b = pl.program_id(0)
    length = out.shape[-1]
    if from_baselines:
        fl = ins[0].shape[2]
        for kz, block in enumerate(ins):
            rows = pl.ds(pl.multiple_of((here[1] ^ kz) * fl, fl), fl)
            for c in range(2):
                lined[rows, c * length : (c + 1) * length] = block[c, b].astype(lined.dtype)
    else:
        hb, fs = pl.num_programs(0), ins[0].shape[2]
        fl = fs * count
        for k, block in enumerate(ins):
            for z in range(lined.shape[0] // fl):
                rows = pl.ds(pl.multiple_of(z * fl + (here[0] ^ k) * fs, fs), fs)
                for c in range(2):
                    lined[rows, c * length : (c + 1) * length] = block[c, z * hb + b].astype(lined.dtype)
    total = jnp.dot(bank[0], lined[...].astype(jnp.bfloat16), preferred_element_type=jnp.float32)
    for c in range(2):
        out[c, 0] = total[:, c * length : (c + 1) * length].astype(jnp.bfloat16)


def delay_filter(classes, here, bank, blocks, half, hb, out_shape, before, from_baselines):
    _, channels, _ = bank.shape
    length = out_shape[-1]
    fixed = [pl.BlockSpec(b.shape, lambda i, classes, here: (0, 0, 0, 0)) for b in blocks]
    specs = [pl.BlockSpec((1, channels, channels), lambda i, classes, here: (classes[half * hb + i], 0, 0))] + fixed
    operands = [bank] + list(blocks)
    aliases = {}
    if before is not None:
        specs.append(pl.BlockSpec(memory_space=pl.ANY))
        operands.append(before)
        aliases = {2 + len(operands) - 1: 0}
    out = jax.ShapeDtypeStruct(out_shape, jnp.bfloat16)
    return pl.pallas_call(
        functools.partial(
            filter_kernel, count=len(blocks), from_baselines=from_baselines, aliased=int(before is not None)
        ),
        out_shape=out,
        grid_spec=pltpu.PrefetchScalarGridSpec(
            num_scalar_prefetch=2,
            grid=(hb,),
            in_specs=specs,
            out_specs=pl.BlockSpec((2, 1, channels, length), lambda i, classes, here: (0, half * hb + i, 0, 0)),
            scratch_shapes=[pltpu.VMEM((channels, 2 * length), row_type(blocks[0].shape[2]))],
        ),
        input_output_aliases=aliases,
        compiler_params=params(),
        cost_estimate=cost(4 * hb * length * channels**2, list(blocks) + [out]),
    )(classes, here, *operands)


def shards(
    visibility,
    spectrum_power_sum,
    square_sum,
    accum_count,
    rfi_mask,
    baseline_delay_class,
    filter_bank,
):
    n, z_count = lax.axis_size("tm"), lax.axis_size("freq")
    parts, baselines, fl, length = visibility.shape
    fs, hb = fl // n, baselines // z_count // 2
    here = jnp.stack([lax.axis_index("tm"), lax.axis_index("freq")]).astype(jnp.int32)
    classes = baseline_delay_class[:, 0]
    smooth = smoothing_weights(spectrum_power_sum, square_sum, accum_count, rfi_mask)
    vis = visibility.reshape(parts, z_count, 2, hb, fl, length)
    by_channel = [(parts, z_count * hb, fs, length)] * n
    by_baseline = [(parts, hb, fl, length)] * z_count
    out_shape = (parts, 2 * hb, fl * z_count, length)

    late = weigh(weigh_by_baseline, here, vis, smooth, 1, by_baseline)
    late = exchange(late, "freq")
    early = weigh(weigh_by_channel, here, vis, smooth, 0, by_channel)
    early = transform_call(here, exchange(early, "tm"))
    early = repack(channels_to_baselines, here, exchange(early, "tm"), by_baseline, z_count)
    early = exchange(early, "freq")

    late = repack(baselines_to_channels, here, late, by_channel, z_count)
    late = transform_call(here, exchange(late, "tm"))
    late = exchange(late, "tm")
    filtered = delay_filter(classes, here, filter_bank, early, 0, hb, out_shape, None, True)
    return delay_filter(classes, here, filter_bank, late, 1, hb, out_shape, filtered, False)


def solution(mesh):
    in_specs = (
        P(None, None, "freq", "tm"),
        P("freq", "tm"),
        P("freq", "tm"),
        P("freq", "tm"),
        P("freq", "tm"),
        P("freq", None),
        P(),
    )
    out_specs = P(None, "freq", None, "tm")
    return jax.shard_map(shards, mesh=mesh, in_specs=in_specs, out_specs=out_specs, check_vma=False)
```

```python
import functools
import math

import jax
import jax.numpy as jnp
import ml_dtypes
import numpy as np
from jax import lax
from jax.experimental import pallas as pl
from jax.experimental.pallas import tpu as pltpu
from jax.sharding import PartitionSpec as P

RIM = 16
LANES = 128
VMEM_BYTES = 20 * 1024 * 1024

WHOLE = pl.BlockSpec(memory_space=pltpu.VMEM)
ANYWHERE = pl.BlockSpec(memory_space=pl.ANY)
SCALARS = pl.BlockSpec(memory_space=pltpu.SMEM)


def row_type(rows):
    return jnp.bfloat16 if rows % 16 == 0 else jnp.float32


def row_type(rows):
    return jnp.bfloat16 if rows % 16 == 0 else jnp.float32


def params():
    return pltpu.CompilerParams(vmem_limit_bytes=VMEM_BYTES)


def cost(flops, arrays):
    return pl.CostEstimate(flops=flops, bytes_accessed=sum(a.size * a.dtype.itemsize for a in arrays), transcendentals=0)


def swap(value, axis, k):
    size = lax.axis_size(axis)
    return lax.ppermute(value, axis, [(i, i ^ k) for i in range(size)])


def exchange(blocks, axis):
    order = sorted(range(1, len(blocks)), key=lambda k: (-bin(k >> 1).count("1"), k))
    moved = {0: blocks[0]}
    for k in order:
        moved[k] = swap(blocks[k], axis, k)
    return [moved[k] for k in range(len(blocks))]


def exchange_both(packed):
    flat = packed.reshape((-1,) + packed.shape[2:])
    return lax.all_to_all(flat, ("tm", "freq"), 0, 0, tiled=True).reshape(packed.shape)


def smoothing_weights(spectrum_power_sum, square_sum, accum_count, rfi_mask):
    counts = accum_count.astype(jnp.float32)
    kurtosis = (
        (counts + 1.0)
        / (counts - 1.0)
        * (counts * square_sum / (spectrum_power_sum * spectrum_power_sum) - 1.0)
    )
    flag_weight = rfi_mask.astype(jnp.float32) * jnp.exp(-2.0 * (kurtosis - 1.0) ** 2)
    devices, length = lax.axis_size("tm"), flag_weight.shape[1]
    up = [(i, (i + 1) % devices) for i in range(devices)]
    before = lax.ppermute(flag_weight[:, length - RIM :], "tm", up)
    after = lax.ppermute(flag_weight[:, :RIM], "tm", [(j, i) for i, j in up])
    padded = jnp.concatenate([before, flag_weight, after], axis=1)
    smooth_weight = jnp.zeros(flag_weight.shape, jnp.float32)
    for offset in range(2 * RIM + 1):
        factor = (RIM + 1 - abs(offset - RIM)) / float((RIM + 1) ** 2)
        smooth_weight = smooth_weight + factor * padded[:, offset : offset + length]
    return smooth_weight


def weigh_by_both(here, vis, smooth, _, out):
    n, z_count, _, hb, fs, _ = out.shape
    for z in range(z_count):
        for c in range(2):
            for b in range(hb):
                value = (vis[c, z, 0, b].astype(jnp.float32) * smooth[...]).astype(jnp.bfloat16)
                for t in range(n):
                    out[t, z, c, b] = value[t * fs : (t + 1) * fs]


def weigh_by_channel(here, vis, smooth, _, *outs):
    me = here[0]
    fs = vis.shape[4] // len(outs)
    for k, out in enumerate(outs):
        rows = pl.ds(pl.multiple_of((me ^ k) * fs, fs), fs)
        part = smooth[rows, :]
        for c in range(2):
            for z in range(vis.shape[1]):
                for b in range(vis.shape[3]):
                    out[c, z * vis.shape[3] + b] = (vis[c, z, 0, b, rows, :].astype(jnp.float32) * part).astype(jnp.bfloat16)


def weigh(kernel, here, after, vis, smooth, half, shapes):
    parts, z, _, hb, fl, length = vis.shape
    block = pl.BlockSpec((parts, z, 1, hb, fl, length), lambda i: (0, 0, half, 0, 0, 0))
    fixed = pl.BlockSpec((fl, length), lambda i: (0, 0))
    outs = [jax.ShapeDtypeStruct(s, jnp.bfloat16) for s in shapes]
    return pl.pallas_call(
        kernel,
        grid=(1,),
        out_shape=outs,
        in_specs=[SCALARS, block, fixed, ANYWHERE],
        out_specs=[pl.BlockSpec(s, lambda i, dims=len(s): (0,) * dims) for s in shapes],
        compiler_params=params(),
        cost_estimate=cost(0, outs + outs),
    )(here, vis, smooth, after)


def transform_tables(n, length):
    group = length // n
    lane = np.arange(length)
    order = np.zeros((length, length))
    order[lane, (lane % n) * group + lane // n] = 1.0
    angle = 2.0 * np.pi / length * (np.outer(lane, lane) % length)
    cosine, sine = np.cos(angle), np.sin(angle)
    table = np.block([[cosine, -sine], [sine, cosine]])
    high = table.astype(ml_dtypes.bfloat16)
    low = (table - high.astype(np.float64)).astype(ml_dtypes.bfloat16)
    turn = 2.0 * np.pi / (n * length) * np.outer(np.arange(n), lane)
    scale = 1.0 / math.sqrt(n * length)
    twiddle = np.stack([np.cos(turn), np.sin(turn)]) * scale
    return order.astype(ml_dtypes.bfloat16), high, low, twiddle.astype(np.float32)


def short_dft(values):
    n = len(values)
    if n == 1:
        return values
    even, odd = short_dft(values[0::2]), short_dft(values[1::2])
    out = [None] * n
    for k in range(n // 2):
        real, imag = odd[k]
        if 4 * k == n:
            real, imag = imag, -real
        elif k:
            c, s = math.cos(2.0 * math.pi * k / n), math.sin(2.0 * math.pi * k / n)
            if 8 * k == n:
                real, imag = c * (real + imag), c * (imag - real)
            elif 8 * k == 3 * n:
                real, imag = s * (imag - real), -s * (real + imag)
            else:
                real, imag = c * real + s * imag, c * imag - s * real
        out[k] = (even[k][0] + real, even[k][1] + imag)
        out[k + n // 2] = (even[k][0] - real, even[k][1] - imag)
    return out


def transpose_groups(values, group):
    values, n = [list(v) for v in values], len(values)
    lane = lax.broadcasted_iota(jnp.int32, values[0][0].shape, 1)
    bit = n // 2
    while bit:
        shift = bit * group
        for i in range(n):
            if i & bit:
                continue
            a, b = values[i], values[i + bit]
            if shift >= LANES:
                step = shift // LANES
                for col in range(len(a)):
                    if not col & step:
                        a[col + step], b[col] = b[col], a[col + step]
            else:
                upper = (lane & shift) != 0
                for col in range(len(a)):
                    x, y = a[col], b[col]
                    a[col] = jnp.where(upper, pltpu.roll(y, shift, 1), x)
                    b[col] = jnp.where(upper, y, pltpu.roll(x, LANES - shift, 1))
        bit //= 2
    return values


def transform(here, _, order, high, low, twiddle, *refs, n, first):
    blocks, packed = (refs[:n], refs[n]) if first else (refs[1 : n + 1], refs[0])
    ordered, lined, stage, done = refs[n + 1 :]
    me = here[0]
    _, z_count, parts, hb, fs, length = packed.shape
    planes = z_count * hb
    group, cols = length // n, length // LANES
    per = lined.shape[1] // fs
    zs = per // hb

    def step(i, carry):
        for c in range(parts):
            for k in range(n):
                if first:
                    block = blocks[k][c, pl.ds(i * per, per)].reshape(per * fs, length)
                    target = me ^ k
                else:
                    block = packed[k, pl.ds(i * zs, zs), c].reshape(per * fs, length)
                    target = k
                ordered[target] = jnp.dot(block, order[...], preferred_element_type=jnp.float32)
            for r in range(0, per * fs, 16):
                values = [[ordered[p, r : r + 16, q * LANES : (q + 1) * LANES] for q in range(cols)] for p in range(n)]
                for v, columns in enumerate(transpose_groups(values, group)):
                    for q, column in enumerate(columns):
                        lined[v, r : r + 16, c * length + q * LANES : c * length + (q + 1) * LANES] = column.astype(jnp.bfloat16)
        flat = lined[...].reshape(n * per * fs, 2 * length)
        total = jnp.dot(flat, high[...], preferred_element_type=jnp.float32)
        total = total + jnp.dot(flat, low[...], preferred_element_type=jnp.float32)
        stage[...] = total.reshape(n, per * fs, 2 * length)
        for r in range(0, per * fs, 16):
            for q in range(cols):
                left, right = slice(q * LANES, (q + 1) * LANES), slice(length + q * LANES, length + (q + 1) * LANES)
                turned = []
                for v in range(n):
                    real, imag = stage[v, r : r + 16, left], stage[v, r : r + 16, right]
                    c, s = twiddle[0, v : v + 1, left], twiddle[1, v : v + 1, left]
                    turned.append((real * c + imag * s, imag * c - real * s))
                for m, pair in enumerate(short_dft(turned)):
                    for c in range(2):
                        done[m, c, r : r + 16, left] = pair[c].astype(jnp.bfloat16)
        for k in range(n):
            for c in range(2):
                if first:
                    packed[k, pl.ds(i * zs, zs), c] = done[k, c].reshape(zs, hb, fs, length)
                else:
                    blocks[k][c, pl.ds(i * per, per)] = done[me ^ k, c].reshape(per, fs, length)
        return carry

    lax.fori_loop(0, planes // per, step, 0)


def transform_call(here, after, blocks, out_shapes, first):
    n, z_count, parts, hb, fs, length = out_shapes[0] if first else blocks[0].shape
    planes = z_count * hb
    per = math.gcd(planes, 4)
    rows = per * fs
    tables = transform_tables(n, length)
    outs = [jax.ShapeDtypeStruct(s, jnp.bfloat16) for s in out_shapes]
    return pl.pallas_call(
        functools.partial(transform, n=n, first=first),
        out_shape=outs,
        in_specs=[SCALARS, ANYWHERE] + [WHOLE] * (4 + len(blocks)),
        out_specs=[WHOLE] * len(outs),
        scratch_shapes=[
            pltpu.VMEM((n, rows, length), jnp.float32),
            pltpu.VMEM((n, rows, 2 * length), jnp.bfloat16),
            pltpu.VMEM((n, rows, 2 * length), jnp.float32),
            pltpu.VMEM((n, 2, rows, length), jnp.bfloat16),
        ],
        compiler_params=params(),
        cost_estimate=cost(4 * n * planes * fs * (2 * length) ** 2, list(blocks) + outs),
    )(here, after, *[jnp.asarray(t) for t in tables], *blocks)


def filter_kernel(classes, here, bank, *refs, count, packed, aliased):
    ins, out, lined = refs[:count], refs[count + aliased], refs[-1]
    b = pl.program_id(0)
    length = out.shape[-1]
    if packed:
        n, z_count, _, _, fs, _ = ins[0].shape
        for t in range(n):
            for z in range(z_count):
                rows = slice((z * n + t) * fs, (z * n + t + 1) * fs)
                for c in range(2):
                    lined[rows, c * length : (c + 1) * length] = ins[0][t, z, c, b].astype(lined.dtype)
    else:
        hb, fs = pl.num_programs(0), ins[0].shape[2]
        fl = fs * count
        for k, block in enumerate(ins):
            for z in range(lined.shape[0] // fl):
                rows = pl.ds(pl.multiple_of(z * fl + (here[0] ^ k) * fs, fs), fs)
                for c in range(2):
                    lined[rows, c * length : (c + 1) * length] = block[c, z * hb + b].astype(lined.dtype)
    total = jnp.dot(bank[0], lined[...].astype(jnp.bfloat16), preferred_element_type=jnp.float32)
    for c in range(2):
        out[c, 0] = total[:, c * length : (c + 1) * length].astype(jnp.bfloat16)


def delay_filter(classes, here, bank, blocks, half, hb, out_shape, before, packed):
    _, channels, _ = bank.shape
    length = out_shape[-1]
    fixed = [pl.BlockSpec(b.shape, lambda i, classes, here, dims=len(b.shape): (0,) * dims) for b in blocks]
    specs = [pl.BlockSpec((1, channels, channels), lambda i, classes, here: (classes[half * hb + i], 0, 0))] + fixed
    operands = [bank] + list(blocks)
    aliases = {}
    if before is not None:
        specs.append(pl.BlockSpec(memory_space=pl.ANY))
        operands.append(before)
        aliases = {2 + len(operands) - 1: 0}
    out = jax.ShapeDtypeStruct(out_shape, jnp.bfloat16)
    return pl.pallas_call(
        functools.partial(
            filter_kernel, count=len(blocks), packed=packed, aliased=int(before is not None)
        ),
        out_shape=out,
        grid_spec=pltpu.PrefetchScalarGridSpec(
            num_scalar_prefetch=2,
            grid=(hb,),
            in_specs=specs,
            out_specs=pl.BlockSpec((2, 1, channels, length), lambda i, classes, here: (0, half * hb + i, 0, 0)),
            scratch_shapes=[pltpu.VMEM((channels, 2 * length), row_type(blocks[0].shape[2]))],
        ),
        input_output_aliases=aliases,
        compiler_params=params(),
        cost_estimate=cost(4 * hb * length * channels**2, list(blocks) + [out]),
    )(classes, here, *operands)


def shards(
    visibility,
    spectrum_power_sum,
    square_sum,
    accum_count,
    rfi_mask,
    baseline_delay_class,
    filter_bank,
):
    n, z_count = lax.axis_size("tm"), lax.axis_size("freq")
    parts, baselines, fl, length = visibility.shape
    fs, hb = fl // n, baselines // z_count // 2
    here = jnp.stack([lax.axis_index("tm"), lax.axis_index("freq")]).astype(jnp.int32)
    classes = baseline_delay_class[:, 0]
    smooth = smoothing_weights(spectrum_power_sum, square_sum, accum_count, rfi_mask)
    vis = visibility.reshape(parts, z_count, 2, hb, fl, length)
    by_channel = [(parts, z_count * hb, fs, length)] * n
    by_both = [(n, z_count, parts, hb, fs, length)]
    out_shape = (parts, 2 * hb, fl * z_count, length)

    (late_out,) = weigh(weigh_by_both, here, smooth, vis, smooth, 1, by_both)
    late = exchange_both(late_out)
    early_out = weigh(weigh_by_channel, here, late_out, vis, smooth, 0, by_channel)
    early_out = transform_call(here, early_out[0], exchange(early_out, "tm"), by_both, True)
    early = exchange_both(early_out[0])
    late_out = transform_call(here, early_out[0], [late], by_channel, False)
    late = exchange(late_out, "tm")
    filtered = delay_filter(classes, here, filter_bank, late, 1, hb, out_shape, None, False)
    return delay_filter(classes, here, filter_bank, [early], 0, hb, out_shape, filtered, True)


def solution(mesh):
    in_specs = (
        P(None, None, "freq", "tm"),
        P("freq", "tm"),
        P("freq", "tm"),
        P("freq", "tm"),
        P("freq", "tm"),
        P("freq", None),
        P(),
    )
    out_specs = P(None, "freq", None, "tm")
    return jax.shard_map(shards, mesh=mesh, in_specs=in_specs, out_specs=out_specs, check_vma=False)
```

```python
import functools
import math

import jax
import jax.numpy as jnp
import ml_dtypes
import numpy as np
from jax import lax
from jax.experimental import pallas as pl
from jax.experimental.pallas import tpu as pltpu
from jax.sharding import PartitionSpec as P

RIM = 16
LANES = 128
VMEM_BYTES = 20 * 1024 * 1024
MOST_VMEM_BYTES = 60 * 1024 * 1024

WHOLE = pl.BlockSpec(memory_space=pltpu.VMEM)
ANYWHERE = pl.BlockSpec(memory_space=pl.ANY)
SCALARS = pl.BlockSpec(memory_space=pltpu.SMEM)


def row_type(rows):
    return jnp.bfloat16 if rows % 16 == 0 else jnp.float32


def row_type(rows):
    return jnp.bfloat16 if rows % 16 == 0 else jnp.float32


def fixed(array):
    return pl.BlockSpec(array.shape, lambda i, dims=len(array.shape): (0,) * dims)


def params(limit=VMEM_BYTES):
    return pltpu.CompilerParams(vmem_limit_bytes=limit)


def cost(flops, arrays):
    return pl.CostEstimate(flops=flops, bytes_accessed=sum(a.size * a.dtype.itemsize for a in arrays), transcendentals=0)


def swap(value, axis, k):
    size = lax.axis_size(axis)
    return lax.ppermute(value, axis, [(i, i ^ k) for i in range(size)])


def exchange(blocks, axis):
    order = sorted(range(1, len(blocks)), key=lambda k: (-bin(k >> 1).count("1"), k))
    moved = {0: blocks[0]}
    for k in order:
        moved[k] = swap(blocks[k], axis, k)
    return [moved[k] for k in range(len(blocks))]


def exchange_both(packed):
    flat = packed.reshape((-1,) + packed.shape[2:])
    return lax.all_to_all(flat, ("tm", "freq"), 0, 0, tiled=True).reshape(packed.shape)


def flag_weights(spectrum_power_sum, square_sum, accum_count, rfi_mask):
    counts = accum_count.astype(jnp.float32)
    kurtosis = (
        (counts + 1.0)
        / (counts - 1.0)
        * (counts * square_sum / (spectrum_power_sum * spectrum_power_sum) - 1.0)
    )
    return rfi_mask.astype(jnp.float32) * jnp.exp(-2.0 * (kurtosis - 1.0) ** 2)


def taps(source, target):
    return np.maximum(RIM + 1 - np.abs(np.asarray(source)[:, None] - np.asarray(target)[None, :]), 0)


def smoothing_table(length, margin):
    return taps(np.arange(-margin, length + margin), np.arange(length)).astype(ml_dtypes.bfloat16)


def ends_tables(length):
    lane = np.arange(length)
    ends = np.concatenate([lane[: 2 * RIM], lane[length - 2 * RIM :]])
    outer = (lane < RIM) | (lane >= length - RIM)
    picked = (lane[:, None] == ends[None, :]).astype(np.float32)
    none = np.zeros_like(picked)
    pick = np.stack([np.concatenate([picked, none], 1), np.concatenate([none, picked], 1)])
    near = [np.tile(taps(ends + shift * length, lane) * outer, (2, 1)) for shift in (-1, 0, 1)]
    return pick.astype(ml_dtypes.bfloat16), np.concatenate(near).astype(ml_dtypes.bfloat16)


def smoothed(parts, table):
    total = sum(jnp.dot(part, table, preferred_element_type=jnp.float32) for part in parts)
    return total * (1.0 / (RIM + 1) ** 2)


def in_parts(value, count):
    parts = []
    for _ in range(count):
        parts.append(value.astype(jnp.bfloat16))
        value = value - parts[-1].astype(jnp.float32)
    return parts


def weigh_by_both(vis, flag_weight, table, pick, _, out, smooth, ends):
    n, _, planes, fs, _ = out.shape
    _, _, _, hb, fl, length = vis.shape
    cols = length // LANES

    @pl.when(pl.program_id(0) == 0)
    def _():
        lane = lax.broadcasted_iota(jnp.int32, (fl, length), 1)
        inside = (lane >= RIM) & (lane < length - RIM)
        smooth[...] = jnp.where(inside, smoothed(in_parts(flag_weight[...], 3), table[...]), 1.0)
        high, low = in_parts(flag_weight[...], 2)
        picked = jnp.dot(high, pick[0], preferred_element_type=jnp.float32)
        picked = picked + jnp.dot(low, pick[1], preferred_element_type=jnp.float32)
        ends[...] = picked.astype(jnp.bfloat16)

    for t in range(n):
        out[t, 0, planes - 1] = ends[t * fs : (t + 1) * fs]
    for c in range(2):
        for b in range(hb):
            value = (vis[c, 0, 0, b].astype(jnp.float32) * smooth[...]).astype(jnp.bfloat16)
            for t in range(n):
                for q in range(cols):
                    out[t, 0, (c * hb + b) * cols + q] = value[t * fs : (t + 1) * fs, q * LANES : (q + 1) * LANES]


def weigh(after, vis, flag_weight, half, n):
    parts, z_count, _, hb, fl, length = vis.shape
    fs, planes = fl // n, parts * hb * (length // LANES) + 1
    small = (flag_weight, jnp.asarray(smoothing_table(length, 0)), jnp.asarray(ends_tables(length)[0]))
    out = jax.ShapeDtypeStruct((n, z_count, planes, fs, LANES), jnp.bfloat16)
    return pl.pallas_call(
        weigh_by_both,
        grid=(z_count,),
        out_shape=out,
        in_specs=[pl.BlockSpec((parts, 1, 1, hb, fl, length), lambda i: (0, i, half, 0, 0, 0))]
        + [fixed(a) for a in small]
        + [ANYWHERE],
        out_specs=pl.BlockSpec((n, 1, planes, fs, LANES), lambda i: (0, i, 0, 0, 0)),
        scratch_shapes=[pltpu.VMEM((fl, length), jnp.float32), pltpu.VMEM((fl, LANES), jnp.bfloat16)],
        compiler_params=params(),
        cost_estimate=cost(0, [out, out]),
    )(vis, *small, after)


def pack_by_channel(here, vis, flag_weight, _, *outs):
    fs, hb = outs[0].shape[1], vis.shape[3]
    for k, out in enumerate(outs):
        rows = pl.ds(pl.multiple_of((here[0] ^ k) * fs, fs), fs)
        value = flag_weight[rows, :]
        high = value.astype(jnp.bfloat16)
        out[out.shape[0] - 2] = high
        out[out.shape[0] - 1] = (value - high.astype(jnp.float32)).astype(jnp.bfloat16)
        for c in range(2):
            for z in range(vis.shape[1]):
                for b in range(hb):
                    out[(c * vis.shape[1] + z) * hb + b] = vis[c, z, 0, b, rows, :]


def pack(kernel, here, after, vis, smooth, half, shapes):
    parts, z, _, hb, fl, length = vis.shape
    block = pl.BlockSpec((parts, z, 1, hb, fl, length), lambda i: (0, 0, half, 0, 0, 0))
    fixed = pl.BlockSpec((fl, length), lambda i: (0, 0))
    outs = [jax.ShapeDtypeStruct(s, jnp.bfloat16) for s in shapes]
    return pl.pallas_call(
        kernel,
        grid=(1,),
        out_shape=outs,
        in_specs=[SCALARS, block, fixed, ANYWHERE],
        out_specs=[pl.BlockSpec(s, lambda i, dims=len(s): (0,) * dims) for s in shapes],
        compiler_params=params(),
        cost_estimate=cost(0, outs + outs),
    )(here, vis, smooth, after)


def transform_tables(n, length):
    group = length // n
    lane = np.arange(length)
    order = np.zeros((n, length, length))
    for p in range(n):
        order[p, lane, (lane % n + p) % n * group + lane // n] = 1.0
    angle = 2.0 * np.pi / length * (np.outer(lane, lane) % length)
    cosine, sine = np.cos(angle), np.sin(angle)
    table = np.block([[cosine, -sine], [sine, cosine]])
    high = table.astype(ml_dtypes.bfloat16)
    low = (table - high.astype(np.float64)).astype(ml_dtypes.bfloat16)
    turn = 2.0 * np.pi / (n * length) * (np.outer(np.arange(n), lane) * (1 - length) % (n * length))
    scale = 1.0 / math.sqrt(n * length)
    twiddle = np.stack([np.cos(turn), np.sin(turn)]) * scale
    return order.astype(ml_dtypes.bfloat16), high, low, twiddle.astype(np.float32)


def short_dft(values):
    n = len(values)
    if n == 1:
        return values
    even, odd = short_dft(values[0::2]), short_dft(values[1::2])
    out = [None] * n
    for k in range(n // 2):
        real, imag = odd[k]
        if 4 * k == n:
            real, imag = imag, -real
        elif k:
            c, s = math.cos(2.0 * math.pi * k / n), math.sin(2.0 * math.pi * k / n)
            if 8 * k == n:
                real, imag = c * (real + imag), c * (imag - real)
            elif 8 * k == 3 * n:
                real, imag = s * (imag - real), -s * (real + imag)
            else:
                real, imag = c * real + s * imag, c * imag - s * real
        out[k] = (even[k][0] + real, even[k][1] + imag)
        out[k + n // 2] = (even[k][0] - real, even[k][1] - imag)
    return out


def gather_groups(values, group):
    n = len(values)
    lane = lax.broadcasted_iota(jnp.int32, values[0][0].shape, 1)
    bit = 1
    while bit < n:
        span = bit * group
        if span >= LANES:
            pick = lambda q, x, y: y if q * LANES & span else x
        else:
            upper = (lane & span) != 0
            pick = lambda q, x, y: jnp.where(upper, y, x)
        values = [[pick(q, x, y) for q, (x, y) in enumerate(zip(values[i], values[(i + bit) % n]))] for i in range(n)]
        bit *= 2
    return [values[-v % n] for v in range(n)]


def transform(here, _, order, high, low, twiddle, near, *refs, n, first, hb):
    blocks, packed = (refs[:n], refs[n]) if first else (refs[1 : n + 1], refs[0])
    ready, ordered, lined, stage, done, wide, smooth = refs[n + 1 :]
    i, me = pl.program_id(0), here[0]
    zs, fs = packed.shape[1], smooth.shape[2]
    rows, length = ready.shape[2:]
    per = zs * hb
    planes = per * pl.num_programs(0)
    group, cols = length // n, length // LANES

    if first:

        @pl.when(i == 0)
        def _():
            for k, block in enumerate(blocks):
                last, p = block.shape[0], me ^ k
                for part in range(2):
                    value = block[last - 2 + part]
                    wide[part, p, :, LANES : LANES + length] = value
                    wide[part, (p + 1) % n, :, :LANES] = value[:, length - LANES :]
                    wide[part, (p + n - 1) % n, :, LANES + length :] = value[:, :LANES]
            parts = [wide[part].reshape(n * fs, length + 2 * LANES) for part in range(2)]
            smooth[0] = smoothed(parts, near[...]).reshape(n, fs, length)

        for k, block in enumerate(blocks):
            weight = smooth[0, me ^ k]
            for c in range(2):
                for j in range(per):
                    value = block[c * planes + i * per + j].astype(jnp.float32) * weight
                    ready[me ^ k, c, j * fs : (j + 1) * fs] = value.astype(jnp.bfloat16)
    else:
        last = packed.shape[2] - 1
        for p in range(n):
            for shift in range(3):
                wide[p, :, :, shift * LANES : (shift + 1) * LANES] = packed[(p + shift - 1) % n, :, last]
        lane = lax.broadcasted_iota(jnp.int32, (n * zs * fs, length), 1)
        inside = (lane >= RIM) & (lane < length - RIM)
        ends = smoothed([wide[...].reshape(n * zs * fs, 3 * LANES)], near[...])
        smooth[...] = jnp.where(inside, 1.0, ends).reshape(n, zs, fs, length)
        for p in range(n):
            for z in range(zs):
                for c in range(2):
                    for b in range(hb):
                        first_row = (z * hb + b) * fs
                        for q in range(cols):
                            lanes = slice(q * LANES, (q + 1) * LANES)
                            value = packed[p, z, (c * hb + b) * cols + q].astype(jnp.float32) * smooth[p, z, :, lanes]
                            ready[p, c, first_row : first_row + fs, lanes] = value.astype(jnp.bfloat16)
    for p in range(n):
        moved = jnp.dot(ready[p].reshape(2 * rows, length), order[p], preferred_element_type=jnp.float32)
        ordered[p] = moved.astype(ordered.dtype).reshape(2, rows, length)
    for c in range(2):
        for r in range(0, rows, 16):
            values = [[ordered[p, c, r : r + 16, q * LANES : (q + 1) * LANES] for q in range(cols)] for p in range(n)]
            for v, columns in enumerate(gather_groups(values, group)):
                for q, column in enumerate(columns):
                    lined[v, r : r + 16, c * length + q * LANES : c * length + (q + 1) * LANES] = column.astype(jnp.bfloat16)
    flat = lined[...].reshape(n * rows, 2 * length)
    total = jnp.dot(flat, high[...], preferred_element_type=jnp.float32)
    total = total + jnp.dot(flat, low[...], preferred_element_type=jnp.float32)
    stage[...] = total.reshape(n, rows, 2 * length)
    for r in range(0, rows, 16):
        for q in range(cols):
            left, right = slice(q * LANES, (q + 1) * LANES), slice(length + q * LANES, length + (q + 1) * LANES)
            turned = []
            for v in range(n):
                real, imag = stage[v, r : r + 16, left], stage[v, r : r + 16, right]
                c, s = twiddle[0, v : v + 1, left], twiddle[1, v : v + 1, left]
                turned.append((real * c + imag * s, imag * c - real * s))
            for m, pair in enumerate(short_dft(turned)):
                for c in range(2):
                    done[m, c, r : r + 16, left] = pair[c].astype(jnp.bfloat16)
    for k in range(n):
        for c in range(2):
            if first:
                packed[k, :, c] = done[k, c].reshape(zs, hb, fs, length)
            else:
                blocks[k][c] = done[me ^ k, c].reshape(per, fs, length)


def transform_call(here, after, blocks, by_both, first):
    n, z_count, parts, hb, fs, length = by_both
    planes = z_count * hb
    steps = max(1, planes // 4)
    per = planes // steps
    rows = per * fs
    zs = per // hb
    near = smoothing_table(length, LANES) if first else ends_tables(length)[1]
    tables = [jnp.asarray(t) for t in transform_tables(n, length) + (near,)]
    if first:
        split = pl.BlockSpec((n, zs, parts, hb, fs, length), lambda i: (0, i, 0, 0, 0, 0))
    else:
        split = pl.BlockSpec((n, zs) + blocks[0].shape[2:], lambda i: (0, i, 0, 0, 0))
    if first:
        outs, out_specs, in_specs = [by_both], [split], [WHOLE] * n
    else:
        outs, in_specs = [(parts, planes, fs, length)] * n, [split]
        out_specs = [pl.BlockSpec((parts, per, fs, length), lambda i: (0, i, 0, 0))] * n
    outs = [jax.ShapeDtypeStruct(s, jnp.bfloat16) for s in outs]
    return pl.pallas_call(
        functools.partial(transform, n=n, first=first, hb=hb),
        grid=(steps,),
        out_shape=outs,
        in_specs=[SCALARS, ANYWHERE] + [WHOLE if first else fixed(t) for t in tables] + in_specs,
        out_specs=out_specs,
        scratch_shapes=[
            pltpu.VMEM((n, 2, rows, length), jnp.bfloat16),
            pltpu.VMEM((n, 2, rows, length), jnp.bfloat16),
            pltpu.VMEM((n, rows, 2 * length), jnp.bfloat16),
            pltpu.VMEM((n, rows, 2 * length), jnp.float32),
            pltpu.VMEM((n, 2, rows, length), jnp.bfloat16),
            pltpu.VMEM((2, n, fs, length + 2 * LANES) if first else (n, zs, fs, 3 * LANES), jnp.bfloat16),
            pltpu.VMEM((1, n, fs, length) if first else (n, zs, fs, length), jnp.float32),
        ],
        compiler_params=params(VMEM_BYTES if first else MOST_VMEM_BYTES),
        cost_estimate=cost(4 * n * planes * fs * (2 * length) ** 2, list(blocks) + outs),
    )(here, after, *tables, *blocks)


def filter_kernel(classes, here, bank, *refs, count, packed, aliased):
    ins, out, lined = refs[:count], refs[count + aliased], refs[-1]
    b = pl.program_id(0)
    length = out.shape[-1]
    if packed:
        n, z_count, _, _, fs, _ = ins[0].shape
        for t in range(n):
            for z in range(z_count):
                rows = slice((z * n + t) * fs, (z * n + t + 1) * fs)
                for c in range(2):
                    lined[rows, c * length : (c + 1) * length] = ins[0][t, z, c, b].astype(lined.dtype)
    else:
        hb, fs = pl.num_programs(0), ins[0].shape[2]
        fl = fs * count
        for k, block in enumerate(ins):
            for z in range(lined.shape[0] // fl):
                rows = pl.ds(pl.multiple_of(z * fl + (here[0] ^ k) * fs, fs), fs)
                for c in range(2):
                    lined[rows, c * length : (c + 1) * length] = block[c, z * hb + b].astype(lined.dtype)
    total = jnp.dot(bank[0], lined[...].astype(jnp.bfloat16), preferred_element_type=jnp.float32)
    for c in range(2):
        out[c, 0] = total[:, c * length : (c + 1) * length].astype(jnp.bfloat16)


def delay_filter(classes, here, bank, blocks, half, hb, out_shape, before, packed):
    _, channels, _ = bank.shape
    length = out_shape[-1]
    fixed = [WHOLE] * len(blocks)
    specs = [pl.BlockSpec((1, channels, channels), lambda i, classes, here: (classes[half * hb + i], 0, 0))] + fixed
    operands = [bank] + list(blocks)
    aliases = {}
    if before is not None:
        specs.append(pl.BlockSpec(memory_space=pl.ANY))
        operands.append(before)
        aliases = {2 + len(operands) - 1: 0}
    out = jax.ShapeDtypeStruct(out_shape, jnp.bfloat16)
    return pl.pallas_call(
        functools.partial(
            filter_kernel, count=len(blocks), packed=packed, aliased=int(before is not None)
        ),
        out_shape=out,
        grid_spec=pltpu.PrefetchScalarGridSpec(
            num_scalar_prefetch=2,
            grid=(hb,),
            in_specs=specs,
            out_specs=pl.BlockSpec((2, 1, channels, length), lambda i, classes, here: (0, half * hb + i, 0, 0)),
            scratch_shapes=[pltpu.VMEM((channels, 2 * length), row_type(blocks[0].shape[2]))],
        ),
        input_output_aliases=aliases,
        compiler_params=params(),
        cost_estimate=cost(4 * hb * length * channels**2, list(blocks) + [out]),
    )(classes, here, *operands)


def shards(
    visibility,
    spectrum_power_sum,
    square_sum,
    accum_count,
    rfi_mask,
    baseline_delay_class,
    filter_bank,
):
    n, z_count = lax.axis_size("tm"), lax.axis_size("freq")
    parts, baselines, fl, length = visibility.shape
    fs, hb = fl // n, baselines // z_count // 2
    here = jnp.stack([lax.axis_index("tm"), lax.axis_index("freq")]).astype(jnp.int32)
    classes = baseline_delay_class[:, 0]
    vis = visibility.reshape(parts, z_count, 2, hb, fl, length)
    planes = z_count * hb
    raw_by_channel = [(parts * planes + 2, fs, length)] * n
    out_shape = (parts, 2 * hb, fl * z_count, length)
    by_both = (n, z_count, parts, hb, fs, length)

    flag_weight = flag_weights(spectrum_power_sum, square_sum, accum_count, rfi_mask)
    early_out = pack(pack_by_channel, here, flag_weight, vis, flag_weight, 0, raw_by_channel)
    early = exchange(early_out, "tm")
    late_out = weigh(early_out[0], vis, flag_weight, 1, n)
    first = (3, 5)
    late_out, *tied = lax.optimization_barrier((late_out, *[early[k] for k in first]))
    for k, value in zip(first, tied):
        early[k] = value
    late = exchange_both(late_out)
    early_out = transform_call(here, late_out, early, by_both, True)
    early = exchange_both(early_out[0])
    late_out = transform_call(here, early_out[0], [late], by_both, False)
    late = exchange(late_out, "tm")
    filtered = delay_filter(classes, here, filter_bank, [early], 0, hb, out_shape, None, True)
    return delay_filter(classes, here, filter_bank, late, 1, hb, out_shape, filtered, False)


def solution(mesh):
    in_specs = (
        P(None, None, "freq", "tm"),
        P("freq", "tm"),
        P("freq", "tm"),
        P("freq", "tm"),
        P("freq", "tm"),
        P("freq", None),
        P(),
    )
    out_specs = P(None, "freq", None, "tm")
    return jax.shard_map(shards, mesh=mesh, in_specs=in_specs, out_specs=out_specs, check_vma=False)
```

```python
import functools
import math

import jax
import jax.numpy as jnp
import ml_dtypes
import numpy as np
from jax import lax
from jax.experimental import pallas as pl
from jax.experimental.pallas import tpu as pltpu
from jax.sharding import PartitionSpec as P

RIM = 16
LANES = 128
VMEM_BYTES = 20 * 1024 * 1024
MOST_VMEM_BYTES = 60 * 1024 * 1024

WHOLE = pl.BlockSpec(memory_space=pltpu.VMEM)
ANYWHERE = pl.BlockSpec(memory_space=pl.ANY)
SCALARS = pl.BlockSpec(memory_space=pltpu.SMEM)


def row_type(rows):
    return jnp.bfloat16 if rows % 16 == 0 else jnp.float32


def row_type(rows):
    return jnp.bfloat16 if rows % 16 == 0 else jnp.float32


def fixed(array):
    return pl.BlockSpec(array.shape, lambda i, dims=len(array.shape): (0,) * dims)


def params(limit=VMEM_BYTES):
    return pltpu.CompilerParams(vmem_limit_bytes=limit)


def cost(flops, arrays):
    return pl.CostEstimate(flops=flops, bytes_accessed=sum(a.size * a.dtype.itemsize for a in arrays), transcendentals=0)


def swap(value, axis, k):
    size = lax.axis_size(axis)
    return lax.ppermute(value, axis, [(i, i ^ k) for i in range(size)])


def exchange(blocks, axis):
    order = sorted(range(1, len(blocks)), key=lambda k: (-bin(k >> 1).count("1"), k))
    moved = {0: blocks[0]}
    for k in order:
        moved[k] = swap(blocks[k], axis, k)
    return [moved[k] for k in range(len(blocks))]


def exchange_both(packed):
    flat = packed.reshape((-1,) + packed.shape[2:])
    return lax.all_to_all(flat, ("tm", "freq"), 0, 0, tiled=True).reshape(packed.shape)


def taps(source, target):
    return np.maximum(RIM + 1 - np.abs(np.asarray(source)[:, None] - np.asarray(target)[None, :]), 0)


def smoothing_table(length):
    return taps(np.arange(length), np.arange(length)).astype(ml_dtypes.bfloat16)


def ends_tables(length):
    lane = np.arange(length)
    ends = np.concatenate([lane[: 2 * RIM], lane[length - 2 * RIM :]])
    outer = (lane < RIM) | (lane >= length - RIM)
    picked = (lane[:, None] == ends[None, :]).astype(np.float32)
    none = np.zeros_like(picked)
    pick = np.stack([np.concatenate([picked, none], 1), np.concatenate([none, picked], 1)])
    near = [np.tile(taps(ends + shift * length, lane) * outer, (2, 1)) for shift in (-1, 0, 1)]
    return pick.astype(ml_dtypes.bfloat16), np.concatenate(near).astype(ml_dtypes.bfloat16)


def smoothed(parts, table):
    total = sum(jnp.dot(part, table, preferred_element_type=jnp.float32) for part in parts)
    return total * (1.0 / (RIM + 1) ** 2)


def in_parts(value, count):
    parts = []
    for _ in range(count):
        parts.append(value.astype(jnp.bfloat16))
        value = value - parts[-1].astype(jnp.float32)
    return parts


def weigh_by_both(vis, power, square, count, mask, table, pick, out, smooth, ends):
    n, _, planes, fs, _ = out.shape
    _, _, _, hb, fl, length = vis.shape
    cols = length // LANES

    @pl.when(pl.program_id(0) == 0)
    def _():
        counts = count[...].astype(jnp.float32)
        total = power[...]
        kurtosis = (counts + 1.0) / (counts - 1.0) * (counts * square[...] / (total * total) - 1.0)
        flag_weight = mask[...].astype(jnp.float32) * jnp.exp(-2.0 * ((kurtosis - 1.0) * (kurtosis - 1.0)))
        lane = lax.broadcasted_iota(jnp.int32, (fl, length), 1)
        inside = (lane >= RIM) & (lane < length - RIM)
        smooth[...] = jnp.where(inside, smoothed(in_parts(flag_weight, 3), table[...]), 1.0)
        high, low = in_parts(flag_weight, 2)
        picked = jnp.dot(high, pick[0], preferred_element_type=jnp.float32)
        picked = picked + jnp.dot(low, pick[1], preferred_element_type=jnp.float32)
        ends[...] = picked.astype(jnp.bfloat16)

    for z in range(out.shape[1]):
        for t in range(n):
            out[t, z, planes - 1] = ends[t * fs : (t + 1) * fs]
        for c in range(2):
            for b in range(hb):
                value = (vis[c, z, 0, b].astype(jnp.float32) * smooth[...]).astype(jnp.bfloat16)
                for t in range(n):
                    for q in range(cols):
                        out[t, z, (c * hb + b) * cols + q] = value[t * fs : (t + 1) * fs, q * LANES : (q + 1) * LANES]


def weigh(vis, fields, half, n):
    parts, z_count, _, hb, fl, length = vis.shape
    fs, planes = fl // n, parts * hb * (length // LANES) + 1
    zs = max(1, z_count // 2)
    small = fields + (jnp.asarray(smoothing_table(length)), jnp.asarray(ends_tables(length)[0]))
    out = jax.ShapeDtypeStruct((n, z_count, planes, fs, LANES), jnp.bfloat16)
    smooth = jax.ShapeDtypeStruct((fl, length), jnp.float32)
    ends = jax.ShapeDtypeStruct((fl, LANES), jnp.bfloat16)
    return pl.pallas_call(
        weigh_by_both,
        grid=(z_count // zs,),
        out_shape=[out, smooth, ends],
        in_specs=[pl.BlockSpec((parts, zs, 1, hb, fl, length), lambda i: (0, i, half, 0, 0, 0))] + [fixed(a) for a in small],
        out_specs=[pl.BlockSpec((n, zs, planes, fs, LANES), lambda i: (0, i, 0, 0, 0)), fixed(smooth), fixed(ends)],
        compiler_params=params(MOST_VMEM_BYTES),
        cost_estimate=cost(0, [out, out]),
    )(vis, *small)


def weigh_by_channel(here, vis, smooth, ends, *outs):
    planes, fs, _ = outs[0].shape
    _, z_count, _, hb, _, length = vis.shape
    cols = length // LANES
    for k, out in enumerate(outs):
        rows = pl.ds(pl.multiple_of((here[0] ^ k) * fs, fs), fs)
        out[planes - 1] = ends[rows, :]
        weight = smooth[rows, :]
        for c in range(2):
            for z in range(z_count):
                for b in range(hb):
                    value = (vis[c, z, 0, b, rows, :].astype(jnp.float32) * weight).astype(jnp.bfloat16)
                    for q in range(cols):
                        out[((c * z_count + z) * hb + b) * cols + q] = value[:, q * LANES : (q + 1) * LANES]


def weigh_early(here, vis, smooth, ends, half, n):
    parts, z_count, _, hb, fl, length = vis.shape
    shape = (parts * z_count * hb * (length // LANES) + 1, fl // n, LANES)
    outs = [jax.ShapeDtypeStruct(shape, jnp.bfloat16)] * n
    return pl.pallas_call(
        weigh_by_channel,
        grid=(1,),
        out_shape=outs,
        in_specs=[SCALARS, pl.BlockSpec((parts, z_count, 1, hb, fl, length), lambda i: (0, 0, half, 0, 0, 0))]
        + [fixed(smooth), fixed(ends)],
        out_specs=[fixed(o) for o in outs],
        compiler_params=params(),
        cost_estimate=cost(0, outs + outs),
    )(here, vis, smooth, ends)


def transform_tables(n, length):
    group = length // n
    lane = np.arange(length)
    order = np.zeros((n, length, length))
    for p in range(n):
        order[p, lane, (lane % n + p) % n * group + lane // n] = 1.0
    angle = 2.0 * np.pi / length * (np.outer(lane, lane) % length)
    cosine, sine = np.cos(angle), np.sin(angle)
    table = np.block([[cosine, -sine], [sine, cosine]])
    high = table.astype(ml_dtypes.bfloat16)
    low = (table - high.astype(np.float64)).astype(ml_dtypes.bfloat16)
    turn = 2.0 * np.pi / (n * length) * (np.outer(np.arange(n), lane) * (1 - length) % (n * length))
    scale = 1.0 / math.sqrt(n * length)
    twiddle = np.stack([np.cos(turn), np.sin(turn)]) * scale
    return order.astype(ml_dtypes.bfloat16), high, low, twiddle.astype(np.float32)


def short_dft(values):
    n = len(values)
    if n == 1:
        return values
    even, odd = short_dft(values[0::2]), short_dft(values[1::2])
    out = [None] * n
    for k in range(n // 2):
        real, imag = odd[k]
        if 4 * k == n:
            real, imag = imag, -real
        elif k:
            c, s = math.cos(2.0 * math.pi * k / n), math.sin(2.0 * math.pi * k / n)
            if 8 * k == n:
                real, imag = c * (real + imag), c * (imag - real)
            elif 8 * k == 3 * n:
                real, imag = s * (imag - real), -s * (real + imag)
            else:
                real, imag = c * real + s * imag, c * imag - s * real
        out[k] = (even[k][0] + real, even[k][1] + imag)
        out[k + n // 2] = (even[k][0] - real, even[k][1] - imag)
    return out


def gather_groups(values, group):
    n = len(values)
    lane = lax.broadcasted_iota(jnp.int32, values[0][0].shape, 1)
    bit = 1
    while bit < n:
        span = bit * group
        if span >= LANES:
            pick = lambda q, x, y: y if q * LANES & span else x
        else:
            upper = (lane & span) != 0
            pick = lambda q, x, y: jnp.where(upper, y, x)
        values = [[pick(q, x, y) for q, (x, y) in enumerate(zip(values[i], values[(i + bit) % n]))] for i in range(n)]
        bit *= 2
    return [values[-v % n] for v in range(n)]


def transform(here, _, order, high, low, twiddle, near, *refs, n, first, hb):
    blocks, packed = (refs[:n], refs[n]) if first else (refs[1 : n + 1], refs[0])
    ready, ordered, lined, stage, done, wide, smooth = refs[n + 1 :]
    i, me = pl.program_id(0), here[0]
    zs, fs = packed.shape[1], smooth.shape[2]
    rows, length = ready.shape[2:]
    per = zs * hb
    planes = per * pl.num_programs(0)
    group, cols = length // n, length // LANES

    def weigh_ends():
        count = smooth.shape[0] * smooth.shape[1] * fs
        lane = lax.broadcasted_iota(jnp.int32, (count, length), 1)
        inside = (lane >= RIM) & (lane < length - RIM)
        ends = smoothed([wide[...].reshape(count, 3 * LANES)], near[...])
        smooth[...] = jnp.where(inside, 1.0, ends).reshape(smooth.shape)

    if first:

        @pl.when(i == 0)
        def _():
            for k, block in enumerate(blocks):
                for shift in range(3):
                    p = lax.rem((me ^ k) + n + 1 - shift, n)
                    wide[p, 0, :, shift * LANES : (shift + 1) * LANES] = block[block.shape[0] - 1]
            weigh_ends()

        for k, block in enumerate(blocks):
            for c in range(2):
                for j in range(per):
                    for q in range(cols):
                        lanes = slice(q * LANES, (q + 1) * LANES)
                        value = block[(c * planes + i * per + j) * cols + q].astype(jnp.float32) * smooth[me ^ k, 0, :, lanes]
                        ready[me ^ k, c, j * fs : (j + 1) * fs, lanes] = value.astype(jnp.bfloat16)
    else:
        last = packed.shape[2] - 1
        for p in range(n):
            for shift in range(3):
                wide[p, :, :, shift * LANES : (shift + 1) * LANES] = packed[(p + shift - 1) % n, :, last]
        weigh_ends()
        for p in range(n):
            for z in range(zs):
                for c in range(2):
                    for b in range(hb):
                        first_row = (z * hb + b) * fs
                        for q in range(cols):
                            lanes = slice(q * LANES, (q + 1) * LANES)
                            value = packed[p, z, (c * hb + b) * cols + q].astype(jnp.float32) * smooth[p, z, :, lanes]
                            ready[p, c, first_row : first_row + fs, lanes] = value.astype(jnp.bfloat16)
    for p in range(n):
        moved = jnp.dot(ready[p].reshape(2 * rows, length), order[p], preferred_element_type=jnp.float32)
        ordered[p] = moved.astype(ordered.dtype).reshape(2, rows, length)
    for c in range(2):
        for r in range(0, rows, 16):
            values = [[ordered[p, c, r : r + 16, q * LANES : (q + 1) * LANES] for q in range(cols)] for p in range(n)]
            for v, columns in enumerate(gather_groups(values, group)):
                for q, column in enumerate(columns):
                    lined[v, r : r + 16, c * length + q * LANES : c * length + (q + 1) * LANES] = column.astype(jnp.bfloat16)
    flat = lined[...].reshape(n * rows, 2 * length)
    total = jnp.dot(flat, high[...], preferred_element_type=jnp.float32)
    total = total + jnp.dot(flat, low[...], preferred_element_type=jnp.float32)
    stage[...] = total.reshape(n, rows, 2 * length)
    for r in range(0, rows, 16):
        for q in range(cols):
            left, right = slice(q * LANES, (q + 1) * LANES), slice(length + q * LANES, length + (q + 1) * LANES)
            turned = []
            for v in range(n):
                real, imag = stage[v, r : r + 16, left], stage[v, r : r + 16, right]
                c, s = twiddle[0, v : v + 1, left], twiddle[1, v : v + 1, left]
                turned.append((real * c + imag * s, imag * c - real * s))
            for m, pair in enumerate(short_dft(turned)):
                for c in range(2):
                    done[m, c, r : r + 16, left] = pair[c].astype(jnp.bfloat16)
    for k in range(n):
        for c in range(2):
            if first:
                packed[k, :, c] = done[k, c].reshape(zs, hb, fs, length)
            else:
                blocks[k][c] = done[me ^ k, c].reshape(per, fs, length)


def transform_call(here, after, blocks, by_both, first):
    n, z_count, parts, hb, fs, length = by_both
    planes = z_count * hb
    steps = max(1, planes // 8)
    per = planes // steps
    rows = per * fs
    zs = per // hb
    tables = [jnp.asarray(t) for t in transform_tables(n, length) + (ends_tables(length)[1],)]
    if first:
        split = pl.BlockSpec((n, zs, parts, hb, fs, length), lambda i: (0, i, 0, 0, 0, 0))
    else:
        split = pl.BlockSpec((n, zs) + blocks[0].shape[2:], lambda i: (0, i, 0, 0, 0))
    if first:
        outs, out_specs, in_specs = [by_both], [split], [WHOLE] * n
    else:
        outs, in_specs = [(parts, planes, fs, length)] * n, [split]
        out_specs = [pl.BlockSpec((parts, per, fs, length), lambda i: (0, i, 0, 0))] * n
    outs = [jax.ShapeDtypeStruct(s, jnp.bfloat16) for s in outs]
    return pl.pallas_call(
        functools.partial(transform, n=n, first=first, hb=hb),
        grid=(steps,),
        out_shape=outs,
        in_specs=[SCALARS, ANYWHERE] + [WHOLE if first else fixed(t) for t in tables] + in_specs,
        out_specs=out_specs,
        scratch_shapes=[
            pltpu.VMEM((n, 2, rows, length), jnp.bfloat16),
            pltpu.VMEM((n, 2, rows, length), jnp.bfloat16),
            pltpu.VMEM((n, rows, 2 * length), jnp.bfloat16),
            pltpu.VMEM((n, rows, 2 * length), jnp.float32),
            pltpu.VMEM((n, 2, rows, length), jnp.bfloat16),
            pltpu.VMEM((n, 1 if first else zs, fs, 3 * LANES), jnp.bfloat16),
            pltpu.VMEM((n, 1 if first else zs, fs, length), jnp.float32),
        ],
        compiler_params=params(VMEM_BYTES if first else MOST_VMEM_BYTES),
        cost_estimate=cost(4 * n * planes * fs * (2 * length) ** 2, list(blocks) + outs),
    )(here, after, *tables, *blocks)


def filter_kernel(classes, here, bank, *refs, count, packed, aliased):
    ins, out, lined = refs[:count], refs[count + aliased], refs[-1]
    b = pl.program_id(0)
    length = out.shape[-1]
    if packed:
        n, z_count, _, _, fs, _ = ins[0].shape
        for t in range(n):
            for z in range(z_count):
                rows = slice((z * n + t) * fs, (z * n + t + 1) * fs)
                for c in range(2):
                    lined[rows, c * length : (c + 1) * length] = ins[0][t, z, c, b].astype(lined.dtype)
    else:
        hb, fs = pl.num_programs(0), ins[0].shape[2]
        fl = fs * count
        for k, block in enumerate(ins):
            for z in range(lined.shape[0] // fl):
                rows = pl.ds(pl.multiple_of(z * fl + (here[0] ^ k) * fs, fs), fs)
                for c in range(2):
                    lined[rows, c * length : (c + 1) * length] = block[c, z * hb + b].astype(lined.dtype)
    total = jnp.dot(bank[0], lined[...].astype(jnp.bfloat16), preferred_element_type=jnp.float32)
    for c in range(2):
        out[c, 0] = total[:, c * length : (c + 1) * length].astype(jnp.bfloat16)


def delay_filter(classes, here, bank, blocks, half, hb, out_shape, before, packed):
    _, channels, _ = bank.shape
    length = out_shape[-1]
    fixed = [WHOLE] * len(blocks)
    specs = [pl.BlockSpec((1, channels, channels), lambda i, classes, here: (classes[half * hb + i], 0, 0))] + fixed
    operands = [bank] + list(blocks)
    aliases = {}
    if before is not None:
        specs.append(pl.BlockSpec(memory_space=pl.ANY))
        operands.append(before)
        aliases = {2 + len(operands) - 1: 0}
    out = jax.ShapeDtypeStruct(out_shape, jnp.bfloat16)
    return pl.pallas_call(
        functools.partial(
            filter_kernel, count=len(blocks), packed=packed, aliased=int(before is not None)
        ),
        out_shape=out,
        grid_spec=pltpu.PrefetchScalarGridSpec(
            num_scalar_prefetch=2,
            grid=(hb,),
            in_specs=specs,
            out_specs=pl.BlockSpec((2, 1, channels, length), lambda i, classes, here: (0, half * hb + i, 0, 0)),
            scratch_shapes=[pltpu.VMEM((channels, 2 * length), row_type(blocks[0].shape[2]))],
        ),
        input_output_aliases=aliases,
        compiler_params=params(),
        cost_estimate=cost(4 * hb * length * channels**2, list(blocks) + [out]),
    )(classes, here, *operands)


def shards(
    visibility,
    spectrum_power_sum,
    square_sum,
    accum_count,
    rfi_mask,
    baseline_delay_class,
    filter_bank,
):
    n, z_count = lax.axis_size("tm"), lax.axis_size("freq")
    parts, baselines, fl, length = visibility.shape
    fs, hb = fl // n, baselines // z_count // 2
    here = jnp.stack([lax.axis_index("tm"), lax.axis_index("freq")]).astype(jnp.int32)
    classes = baseline_delay_class[:, 0]
    vis = visibility.reshape(parts, z_count, 2, hb, fl, length)
    planes = z_count * hb
    out_shape = (parts, 2 * hb, fl * z_count, length)
    by_both = (n, z_count, parts, hb, fs, length)

    late_out, smooth, ends = weigh(vis, (spectrum_power_sum, square_sum, accum_count, rfi_mask), 1, n)
    early_out = weigh_early(here, vis, smooth, ends, 0, n)
    early = exchange(early_out, "tm")
    first = ()
    late_out, *tied = lax.optimization_barrier((late_out, *[early[k] for k in first]))
    for k, value in zip(first, tied):
        early[k] = value
    late = exchange_both(late_out)
    early_out = transform_call(here, late_out, early, by_both, True)
    early = exchange_both(early_out[0])
    late_out = transform_call(here, early_out[0], [late], by_both, False)
    late = exchange(late_out, "tm")
    filtered = delay_filter(classes, here, filter_bank, [early], 0, hb, out_shape, None, True)
    return delay_filter(classes, here, filter_bank, late, 1, hb, out_shape, filtered, False)


def solution(mesh):
    in_specs = (
        P(None, None, "freq", "tm"),
        P("freq", "tm"),
        P("freq", "tm"),
        P("freq", "tm"),
        P("freq", "tm"),
        P("freq", None),
        P(),
    )
    out_specs = P(None, "freq", None, "tm")
    return jax.shard_map(shards, mesh=mesh, in_specs=in_specs, out_specs=out_specs, check_vma=False)
```

```python
import functools
import math

import jax
import jax.numpy as jnp
import ml_dtypes
import numpy as np
from jax import lax
from jax.experimental import pallas as pl
from jax.experimental.pallas import tpu as pltpu
from jax.sharding import PartitionSpec as P

RIM = 16
LANES = 128
VMEM_BYTES = 20 * 1024 * 1024
MOST_VMEM_BYTES = 60 * 1024 * 1024

WHOLE = pl.BlockSpec(memory_space=pltpu.VMEM)
ANYWHERE = pl.BlockSpec(memory_space=pl.ANY)
SCALARS = pl.BlockSpec(memory_space=pltpu.SMEM)


def row_type(rows):
    return jnp.bfloat16 if rows % 16 == 0 else jnp.float32


def row_type(rows):
    return jnp.bfloat16 if rows % 16 == 0 else jnp.float32


def fixed(array):
    return pl.BlockSpec(array.shape, lambda i, dims=len(array.shape): (0,) * dims)


def params(limit=VMEM_BYTES):
    return pltpu.CompilerParams(vmem_limit_bytes=limit)


def cost(flops, arrays):
    return pl.CostEstimate(flops=flops, bytes_accessed=sum(a.size * a.dtype.itemsize for a in arrays), transcendentals=0)


def swap(value, axis, k):
    size = lax.axis_size(axis)
    return lax.ppermute(value, axis, [(i, i ^ k) for i in range(size)])


def exchange(blocks, axis, core_last=False):
    order = sorted(range(1, len(blocks)), key=lambda k: (k == 1, -bin(k >> 1).count("1"), k))
    moved = {0: blocks[0]}
    for k in order:
        block = blocks[k]
        if core_last and k == 1:
            block, moved[order[0]] = lax.optimization_barrier((block, moved[order[0]]))
        moved[k] = swap(block, axis, k)
    return [moved[k] for k in range(len(blocks))]


def exchange_both(packed):
    flat = packed.reshape((-1,) + packed.shape[2:])
    return lax.all_to_all(flat, ("tm", "freq"), 0, 0, tiled=True).reshape(packed.shape)


def taps(source, target):
    return np.maximum(RIM + 1 - np.abs(np.asarray(source)[:, None] - np.asarray(target)[None, :]), 0)


def smoothing_table(length):
    return taps(np.arange(length), np.arange(length)).astype(ml_dtypes.bfloat16)


def ends_tables(length):
    lane = np.arange(length)
    ends = np.concatenate([lane[: 2 * RIM], lane[length - 2 * RIM :]])
    outer = (lane < RIM) | (lane >= length - RIM)
    picked = (lane[:, None] == ends[None, :]).astype(np.float32)
    none = np.zeros_like(picked)
    pick = np.stack([np.concatenate([picked, none], 1), np.concatenate([none, picked], 1)])
    near = [np.tile(taps(ends + shift * length, lane) * outer, (2, 1)) for shift in (-1, 0, 1)]
    return pick.astype(ml_dtypes.bfloat16), np.concatenate(near).astype(ml_dtypes.bfloat16)


def smoothed(parts, table):
    total = sum(jnp.dot(part, table, preferred_element_type=jnp.float32) for part in parts)
    return total * (1.0 / (RIM + 1) ** 2)


def in_parts(value, count):
    parts = []
    for _ in range(count):
        parts.append(value.astype(jnp.bfloat16))
        value = value - parts[-1].astype(jnp.float32)
    return parts


def weigh_by_both(vis, power, square, count, mask, table, pick, out, smooth, ends):
    n, _, planes, fs, _ = out.shape
    _, _, _, hb, fl, length = vis.shape
    cols = length // LANES

    @pl.when(pl.program_id(0) == 0)
    def _():
        counts = count[...].astype(jnp.float32)
        total = power[...]
        kurtosis = (counts + 1.0) / (counts - 1.0) * (counts * square[...] / (total * total) - 1.0)
        flag_weight = mask[...].astype(jnp.float32) * jnp.exp(-2.0 * ((kurtosis - 1.0) * (kurtosis - 1.0)))
        lane = lax.broadcasted_iota(jnp.int32, (fl, length), 1)
        inside = (lane >= RIM) & (lane < length - RIM)
        smooth[...] = jnp.where(inside, smoothed(in_parts(flag_weight, 3), table[...]), 1.0)
        high, low = in_parts(flag_weight, 2)
        picked = jnp.dot(high, pick[0], preferred_element_type=jnp.float32)
        picked = picked + jnp.dot(low, pick[1], preferred_element_type=jnp.float32)
        ends[...] = picked.astype(jnp.bfloat16)

    for z in range(out.shape[1]):
        for t in range(n):
            out[t, z, planes - 1] = ends[t * fs : (t + 1) * fs]
        for c in range(2):
            for b in range(hb):
                value = (vis[c, z, 0, b].astype(jnp.float32) * smooth[...]).astype(jnp.bfloat16)
                for t in range(n):
                    for q in range(cols):
                        out[t, z, (c * hb + b) * cols + q] = value[t * fs : (t + 1) * fs, q * LANES : (q + 1) * LANES]


def weigh(vis, fields, half, n):
    parts, z_count, _, hb, fl, length = vis.shape
    fs, planes = fl // n, parts * hb * (length // LANES) + 1
    zs = max(1, z_count // 2)
    small = fields + (jnp.asarray(smoothing_table(length)), jnp.asarray(ends_tables(length)[0]))
    out = jax.ShapeDtypeStruct((n, z_count, planes, fs, LANES), jnp.bfloat16)
    smooth = jax.ShapeDtypeStruct((fl, length), jnp.float32)
    ends = jax.ShapeDtypeStruct((fl, LANES), jnp.bfloat16)
    return pl.pallas_call(
        weigh_by_both,
        grid=(z_count // zs,),
        out_shape=[out, smooth, ends],
        in_specs=[pl.BlockSpec((parts, zs, 1, hb, fl, length), lambda i: (0, i, half, 0, 0, 0))] + [fixed(a) for a in small],
        out_specs=[pl.BlockSpec((n, zs, planes, fs, LANES), lambda i: (0, i, 0, 0, 0)), fixed(smooth), fixed(ends)],
        compiler_params=params(MOST_VMEM_BYTES),
        cost_estimate=cost(0, [out, out]),
    )(vis, *small)


def weigh_by_channel(here, vis, smooth, ends, *outs):
    planes, fs, _ = outs[0].shape
    _, z_count, _, hb, _, length = vis.shape
    cols = length // LANES
    for k, out in enumerate(outs):
        rows = pl.ds(pl.multiple_of((here[0] ^ k) * fs, fs), fs)
        out[planes - 1] = ends[rows, :]
        weight = smooth[rows, :]
        for c in range(2):
            for z in range(z_count):
                for b in range(hb):
                    value = (vis[c, z, 0, b, rows, :].astype(jnp.float32) * weight).astype(jnp.bfloat16)
                    for q in range(cols):
                        out[((c * z_count + z) * hb + b) * cols + q] = value[:, q * LANES : (q + 1) * LANES]


def weigh_early(here, vis, smooth, ends, half, n):
    parts, z_count, _, hb, fl, length = vis.shape
    shape = (parts * z_count * hb * (length // LANES) + 1, fl // n, LANES)
    outs = [jax.ShapeDtypeStruct(shape, jnp.bfloat16)] * n
    return pl.pallas_call(
        weigh_by_channel,
        grid=(1,),
        out_shape=outs,
        in_specs=[SCALARS, pl.BlockSpec((parts, z_count, 1, hb, fl, length), lambda i: (0, 0, half, 0, 0, 0))]
        + [fixed(smooth), fixed(ends)],
        out_specs=[fixed(o) for o in outs],
        compiler_params=params(),
        cost_estimate=cost(0, outs + outs),
    )(here, vis, smooth, ends)


def transform_tables(n, length):
    group = length // n
    lane = np.arange(length)
    order = np.zeros((n, length, length))
    for p in range(n):
        order[p, lane, (lane % n + p) % n * group + lane // n] = 1.0
    angle = 2.0 * np.pi / length * (np.outer(lane, lane) % length)
    cosine, sine = np.cos(angle), np.sin(angle)
    table = np.block([[cosine, -sine], [sine, cosine]])
    high = table.astype(ml_dtypes.bfloat16)
    low = (table - high.astype(np.float64)).astype(ml_dtypes.bfloat16)
    turn = 2.0 * np.pi / (n * length) * (np.outer(np.arange(n), lane) * (1 - length) % (n * length))
    scale = 1.0 / math.sqrt(n * length)
    twiddle = np.stack([np.cos(turn), np.sin(turn)]) * scale
    return order.astype(ml_dtypes.bfloat16), high, low, twiddle.astype(np.float32)


def short_dft(values):
    n = len(values)
    if n == 1:
        return values
    even, odd = short_dft(values[0::2]), short_dft(values[1::2])
    out = [None] * n
    for k in range(n // 2):
        real, imag = odd[k]
        if 4 * k == n:
            real, imag = imag, -real
        elif k:
            c, s = math.cos(2.0 * math.pi * k / n), math.sin(2.0 * math.pi * k / n)
            if 8 * k == n:
                real, imag = c * (real + imag), c * (imag - real)
            elif 8 * k == 3 * n:
                real, imag = s * (imag - real), -s * (real + imag)
            else:
                real, imag = c * real + s * imag, c * imag - s * real
        out[k] = (even[k][0] + real, even[k][1] + imag)
        out[k + n // 2] = (even[k][0] - real, even[k][1] - imag)
    return out


def gather_groups(values, group):
    n = len(values)
    lane = lax.broadcasted_iota(jnp.int32, values[0][0].shape, 1)
    bit = 1
    while bit < n:
        span = bit * group
        if span >= LANES:
            pick = lambda q, x, y: y if q * LANES & span else x
        else:
            upper = (lane & span) != 0
            pick = lambda q, x, y: jnp.where(upper, y, x)
        values = [[pick(q, x, y) for q, (x, y) in enumerate(zip(values[i], values[(i + bit) % n]))] for i in range(n)]
        bit *= 2
    return [values[-v % n] for v in range(n)]


def transform(here, _, order, high, low, twiddle, near, *refs, n, first, hb):
    blocks, packed = (refs[:n], refs[n]) if first else (refs[1 : n + 1], refs[0])
    ready, ordered, lined, stage, done, wide, smooth = refs[n + 1 :]
    i, me = pl.program_id(0), here[0]
    zs, fs = packed.shape[1], smooth.shape[2]
    rows, length = ready.shape[2:]
    per = zs * hb
    planes = per * pl.num_programs(0)
    group, cols = length // n, length // LANES

    def weigh_ends():
        count = smooth.shape[0] * smooth.shape[1] * fs
        lane = lax.broadcasted_iota(jnp.int32, (count, length), 1)
        inside = (lane >= RIM) & (lane < length - RIM)
        ends = smoothed([wide[...].reshape(count, 3 * LANES)], near[...])
        smooth[...] = jnp.where(inside, 1.0, ends).reshape(smooth.shape)

    if first:

        @pl.when(i == 0)
        def _():
            for k, block in enumerate(blocks):
                for shift in range(3):
                    p = lax.rem((me ^ k) + n + 1 - shift, n)
                    wide[p, 0, :, shift * LANES : (shift + 1) * LANES] = block[block.shape[0] - 1]
            weigh_ends()

        for k, block in enumerate(blocks):
            for c in range(2):
                for j in range(per):
                    for q in range(cols):
                        lanes = slice(q * LANES, (q + 1) * LANES)
                        value = block[(c * planes + i * per + j) * cols + q].astype(jnp.float32) * smooth[me ^ k, 0, :, lanes]
                        ready[me ^ k, c, j * fs : (j + 1) * fs, lanes] = value.astype(jnp.bfloat16)
    else:
        last = packed.shape[2] - 1
        for p in range(n):
            for shift in range(3):
                wide[p, :, :, shift * LANES : (shift + 1) * LANES] = packed[(p + shift - 1) % n, :, last]
        weigh_ends()
        for p in range(n):
            for z in range(zs):
                for c in range(2):
                    for b in range(hb):
                        first_row = (z * hb + b) * fs
                        for q in range(cols):
                            lanes = slice(q * LANES, (q + 1) * LANES)
                            value = packed[p, z, (c * hb + b) * cols + q].astype(jnp.float32) * smooth[p, z, :, lanes]
                            ready[p, c, first_row : first_row + fs, lanes] = value.astype(jnp.bfloat16)
    for p in range(n):
        moved = jnp.dot(ready[p].reshape(2 * rows, length), order[p], preferred_element_type=jnp.float32)
        ordered[p] = moved.astype(ordered.dtype).reshape(2, rows, length)
    for c in range(2):
        for r in range(0, rows, 16):
            values = [[ordered[p, c, r : r + 16, q * LANES : (q + 1) * LANES] for q in range(cols)] for p in range(n)]
            for v, columns in enumerate(gather_groups(values, group)):
                for q, column in enumerate(columns):
                    lined[v, r : r + 16, c * length + q * LANES : c * length + (q + 1) * LANES] = column.astype(jnp.bfloat16)
    flat = lined[...].reshape(n * rows, 2 * length)
    total = jnp.dot(flat, high[...], preferred_element_type=jnp.float32)
    total = total + jnp.dot(flat, low[...], preferred_element_type=jnp.float32)
    stage[...] = total.reshape(n, rows, 2 * length)
    for r in range(0, rows, 16):
        for q in range(cols):
            left, right = slice(q * LANES, (q + 1) * LANES), slice(length + q * LANES, length + (q + 1) * LANES)
            turned = []
            for v in range(n):
                real, imag = stage[v, r : r + 16, left], stage[v, r : r + 16, right]
                c, s = twiddle[0, v : v + 1, left], twiddle[1, v : v + 1, left]
                turned.append((real * c + imag * s, imag * c - real * s))
            for m, pair in enumerate(short_dft(turned)):
                for c in range(2):
                    done[m, c, r : r + 16, left] = pair[c].astype(jnp.bfloat16)
    for k in range(n):
        for c in range(2):
            if first:
                packed[k, :, c] = done[k, c].reshape(zs, hb, fs, length)
            else:
                blocks[k][c] = done[me ^ k, c].reshape(per, fs, length)


def transform_call(here, after, blocks, by_both, first):
    n, z_count, parts, hb, fs, length = by_both
    planes = z_count * hb
    steps = max(1, planes // 8)
    per = planes // steps
    rows = per * fs
    zs = per // hb
    tables = [jnp.asarray(t) for t in transform_tables(n, length) + (ends_tables(length)[1],)]
    if first:
        split = pl.BlockSpec((n, zs, parts, hb, fs, length), lambda i: (0, i, 0, 0, 0, 0))
    else:
        split = pl.BlockSpec((n, zs) + blocks[0].shape[2:], lambda i: (0, i, 0, 0, 0))
    if first:
        outs, out_specs, in_specs = [by_both], [split], [WHOLE] * n
    else:
        outs, in_specs = [(parts, planes, fs, length)] * n, [split]
        out_specs = [pl.BlockSpec((parts, per, fs, length), lambda i: (0, i, 0, 0))] * n
    outs = [jax.ShapeDtypeStruct(s, jnp.bfloat16) for s in outs]
    return pl.pallas_call(
        functools.partial(transform, n=n, first=first, hb=hb),
        grid=(steps,),
        out_shape=outs,
        in_specs=[SCALARS, ANYWHERE] + [WHOLE if first else fixed(t) for t in tables] + in_specs,
        out_specs=out_specs,
        scratch_shapes=[
            pltpu.VMEM((n, 2, rows, length), jnp.bfloat16),
            pltpu.VMEM((n, 2, rows, length), jnp.bfloat16),
            pltpu.VMEM((n, rows, 2 * length), jnp.bfloat16),
            pltpu.VMEM((n, rows, 2 * length), jnp.float32),
            pltpu.VMEM((n, 2, rows, length), jnp.bfloat16),
            pltpu.VMEM((n, 1 if first else zs, fs, 3 * LANES), jnp.bfloat16),
            pltpu.VMEM((n, 1 if first else zs, fs, length), jnp.float32),
        ],
        compiler_params=params(VMEM_BYTES if first else MOST_VMEM_BYTES),
        cost_estimate=cost(4 * n * planes * fs * (2 * length) ** 2, list(blocks) + outs),
    )(here, after, *tables, *blocks)


def copy_kernel(source, target):
    target[...] = source[...]


def hold(array):
    return pl.pallas_call(
        copy_kernel,
        grid=(1,),
        out_shape=jax.ShapeDtypeStruct(array.shape, array.dtype),
        in_specs=[fixed(array)],
        out_specs=WHOLE,
        compiler_params=params(),
        cost_estimate=cost(0, [array, array]),
    )(array)


def filter_kernel(classes, here, bank, *refs, count, packed, aliased):
    ins, out, lined = refs[:count], refs[count + aliased], refs[-1]
    b = pl.program_id(0)
    length = out.shape[-1]
    if packed:
        n, z_count, _, _, fs, _ = ins[0].shape
        for t in range(n):
            for z in range(z_count):
                rows = slice((z * n + t) * fs, (z * n + t + 1) * fs)
                for c in range(2):
                    lined[rows, c * length : (c + 1) * length] = ins[0][t, z, c, b].astype(lined.dtype)
    else:
        hb, fs = pl.num_programs(0), ins[0].shape[2]
        fl = fs * count
        for k, block in enumerate(ins):
            for z in range(lined.shape[0] // fl):
                rows = pl.ds(pl.multiple_of(z * fl + (here[0] ^ k) * fs, fs), fs)
                for c in range(2):
                    lined[rows, c * length : (c + 1) * length] = block[c, z * hb + b].astype(lined.dtype)
    total = jnp.dot(bank[0], lined[...].astype(jnp.bfloat16), preferred_element_type=jnp.float32)
    for c in range(2):
        out[c, 0] = total[:, c * length : (c + 1) * length].astype(jnp.bfloat16)


def delay_filter(classes, here, bank, blocks, half, hb, out_shape, before, packed):
    _, channels, _ = bank.shape
    length = out_shape[-1]
    fixed = [WHOLE] * len(blocks)
    specs = [pl.BlockSpec((1, channels, channels), lambda i, classes, here: (classes[half * hb + i], 0, 0))] + fixed
    operands = [bank] + list(blocks)
    aliases = {}
    if before is not None:
        specs.append(pl.BlockSpec(memory_space=pl.ANY))
        operands.append(before)
        aliases = {2 + len(operands) - 1: 0}
    out = jax.ShapeDtypeStruct(out_shape, jnp.bfloat16)
    return pl.pallas_call(
        functools.partial(
            filter_kernel, count=len(blocks), packed=packed, aliased=int(before is not None)
        ),
        out_shape=out,
        grid_spec=pltpu.PrefetchScalarGridSpec(
            num_scalar_prefetch=2,
            grid=(hb,),
            in_specs=specs,
            out_specs=pl.BlockSpec((2, 1, channels, length), lambda i, classes, here: (0, half * hb + i, 0, 0)),
            scratch_shapes=[pltpu.VMEM((channels, 2 * length), row_type(blocks[0].shape[2]))],
        ),
        input_output_aliases=aliases,
        compiler_params=params(),
        cost_estimate=cost(4 * hb * length * channels**2, list(blocks) + [out]),
    )(classes, here, *operands)


def shards(
    visibility,
    spectrum_power_sum,
    square_sum,
    accum_count,
    rfi_mask,
    baseline_delay_class,
    filter_bank,
):
    n, z_count = lax.axis_size("tm"), lax.axis_size("freq")
    parts, baselines, fl, length = visibility.shape
    fs, hb = fl // n, baselines // z_count // 2
    here = jnp.stack([lax.axis_index("tm"), lax.axis_index("freq")]).astype(jnp.int32)
    classes = baseline_delay_class[:, 0]
    vis = visibility.reshape(parts, z_count, 2, hb, fl, length)
    planes = z_count * hb
    out_shape = (parts, 2 * hb, fl * z_count, length)
    by_both = (n, z_count, parts, hb, fs, length)

    late_out, smooth, ends = weigh(vis, (spectrum_power_sum, square_sum, accum_count, rfi_mask), 1, n)
    early_out = weigh_early(here, vis, smooth, ends, 0, n)
    early = exchange(early_out, "tm")
    first = ()
    late_out, *tied = lax.optimization_barrier((late_out, *[early[k] for k in first]))
    for k, value in zip(first, tied):
        early[k] = value
    late = exchange_both(late_out)
    early_out = transform_call(here, late_out, early, by_both, True)
    early = exchange_both(early_out[0])
    late_out = list(transform_call(here, early_out[0], [late], by_both, False))
    own = hold(late_out[0])
    late_out[1], own = lax.optimization_barrier((late_out[1], own))
    late = [own] + exchange(late_out, "tm", core_last=True)[1:]
    filtered = delay_filter(classes, here, filter_bank, late, 1, hb, out_shape, None, False)
    return delay_filter(classes, here, filter_bank, [early], 0, hb, out_shape, filtered, True)


def solution(mesh):
    in_specs = (
        P(None, None, "freq", "tm"),
        P("freq", "tm"),
        P("freq", "tm"),
        P("freq", "tm"),
        P("freq", "tm"),
        P("freq", None),
        P(),
    )
    out_specs = P(None, "freq", None, "tm")
    return jax.shard_map(shards, mesh=mesh, in_specs=in_specs, out_specs=out_specs, check_vma=False)
```
